32 devices in a mesh: replica: 8 (over z, core), tile: 4 (over y, x).
Axes of the slice: x: 2, y: 2, z: 4, core: 2. Of those that a mesh axis runs over, the one named last changes fastest.
Arguments:
- public_tokens: bfloat16 [2048, 5120], P('replica', 'tile'), may hold values from -6 to 6
- public_targets: bfloat16 [2048, 4096], P(('replica', 'tile')), may hold values from -6 to 6
- private_tokens: bfloat16 [3072, 5120], P('replica', 'tile'), may hold values from -6 to 6
- private_targets: bfloat16 [3072, 4096], P(('replica', 'tile')), may hold values from -6 to 6
- token_counts: int32 [8, 3], P('replica'), may hold values from 1 to 128, 320 in all within a row
- weight: float32 [5120, 4096], P('tile', 'replica'), may hold values from -0.078125 to 0.078125
- public_moment: float32 [5120, 4096], P('tile', 'replica'), may hold values from 1 to 10
- adam_first: float32 [5120, 4096], P('tile', 'replica'), may hold values from -3 to 3
- adam_second: float32 [5120, 4096], P('tile', 'replica'), may hold values from 0.1 to 1
- noise_draw: float32 [5120, 4096], P('tile', 'replica'), may hold values from -6 to 6
Outputs:
- new_weight: float32 [5120, 4096], P('tile', 'replica')
- new_first: float32 [5120, 4096], P('tile', 'replica')
- new_second: float32 [5120, 4096], P('tile', 'replica')
- new_public: float32 [5120, 4096], P('tile', 'replica')
The draws below stay inside these ranges and needn't reach their ends.
Inputs may be any that keep to these rules, and one draw needn't show every extreme that they name: `token_counts`: each row holds the live token counts of one replica's 3 private examples; every row sums to 320 and its largest entry is 128.
All inputs are finite; a program needn't handle non-finite values.
Results may differ from the reference program's by a relative error of at most 0.0031.
Values may be sent and summed in bfloat16 or wider, within the bound.
A program may use at most 128 MiB of HBM per device.

```python
import math
import jax
import jax.numpy as jnp
import numpy as np
from jax import lax

D = 5120
E = 3
L = 128
Q = 4096
PUB = 2048
EXAMPLES = 24
PRIV = 3072
COUNT_SUM = 320
N_REPLICA = 8


def strengthened(entries, own_key, source, target, blocks, factor):
    owner, partner = [(jnp.arange(entries.shape[dim]) // (entries.shape[dim] // blocks)).reshape([-1 if axis == dim else 1 for axis in range(entries.ndim)]) for dim in (source, target)]
    chosen = jax.random.permutation(own_key, blocks)[partner]
    strong = (owner == chosen) | (owner == (partner + blocks // 2) % blocks)
    return jnp.where(strong, factor * entries, entries)


def shard_levels(key, extent, shards, smallest, largest):
    def one(dim, shards_of):
        heights = jax.random.uniform(jax.random.fold_in(jax.random.fold_in(key, 6), dim), (shards_of,), jnp.float32, smallest / len(shards), largest / len(shards))
        return jnp.repeat(jnp.exp(heights), extent[dim] // shards_of).reshape((-1,) + (1,) * (len(extent) - dim - 1))

    gain = one(*shards[0])
    for cut in shards[1:]:
        gain = gain * one(*cut)
    return gain


def split_up(number_of, total, most, skew):
    loads = [(1 << 20) // math.isqrt(standing ** skew) + 1 for standing in range(2, number_of + 1)]
    spare, given = total - most - (number_of - 1), [1] * (number_of - 1)
    while spare > 0:
        movable = [i for i in range(number_of - 1) if given[i] < most]
        pool, left = sum([loads[i] for i in movable]), spare
        for i in movable:
            more = min(most - given[i], max(1, left * loads[i] // pool), spare)
            given[i] = given[i] + more
            spare = spare - more
    return np.array([most] + given)


def uneven_parts(rng, count, total, bound, lean):
    if count == 2:
        one = jax.random.randint(rng, (), max(1, total - bound), min(bound, total - 1) + 1)
        return jnp.stack([one, total - one])
    tallies = jnp.asarray(split_up(count, total, bound, lean), jnp.int32)
    twos = (count - 1) // 2
    donor, taker = tallies[1:1 + 2 * twos:2], tallies[2:2 + 2 * twos:2]
    slack = jnp.minimum(donor - 1, bound - taker)
    moved = jax.random.randint(jax.random.fold_in(rng, 1), (twos,), 0, 1 << 20) % (slack + 1)
    tallies = tallies.at[1:1 + 2 * twos:2].set(donor - moved).at[2:2 + 2 * twos:2].set(taker + moved)
    return tallies[jax.random.permutation(jax.random.fold_in(rng, 2), count)]


def centred(key, shape, spread, limit, cuts=(), kind=jnp.bfloat16):
    level = shard_levels(key, shape, cuts, -0.22, 0.18) if cuts else 1.0
    array = jax.random.normal(key, shape, jnp.float32) * spread * level
    return jnp.minimum(jnp.maximum(array, -limit), limit).astype(kind)


def bell_draw_with(own_key, dims, width, most, split, heavy, held_as=jnp.bfloat16):
    entries = width * jax.random.normal(own_key, dims, jnp.float32)
    if split:
        entries = entries * shard_levels(own_key, dims, split, -0.22, 0.18)
    return jnp.clip(strengthened(entries, jax.random.fold_in(own_key, 3), *heavy), -most, most).astype(held_as)


def setup_inputs(seed: int = 0) -> dict:
    arg_keys = jax.random.split(jax.random.key(seed), 11)
    return {
        "public_tokens": bell_draw_with(arg_keys[0], (PUB, D), 1.0, 6.0, ((0, 8), (1, 4)), (1, 0, 8, 2.0)),
        "public_targets": centred(arg_keys[1], (PUB, Q), 1.0, 6.0, ((0, 32),)),
        "private_tokens": bell_draw_with(arg_keys[2], (PRIV, D), 1.0, 6.0, ((0, 8), (1, 4)), (1, 0, 8, 2.0)),
        "private_targets": centred(arg_keys[3], (PRIV, Q), 1.0, 6.0, ((0, 32),)),
        "token_counts": jax.vmap(lambda own: uneven_parts(own, E, COUNT_SUM, L, 1))(jax.random.split(arg_keys[4], N_REPLICA)).reshape((N_REPLICA, E)).astype(jnp.int32),
        "weight": centred(arg_keys[5], (D, Q), D ** -0.5, 0.078125, ((0, 4), (1, 8)), jnp.float32),
        "public_moment": jnp.clip(jnp.exp(math.log(10.0) - 2.3025851 * jax.random.uniform(arg_keys[6], (D, Q), jnp.float32) ** shard_levels(arg_keys[6], (D, Q), ((0, 4), (1, 8)), -0.2, 0.2)), 1.0, 10.0),
        "adam_first": centred(arg_keys[7], (D, Q), 0.5, 3.0, ((0, 4), (1, 8)), jnp.float32),
        "adam_second": jnp.clip(jnp.exp(math.log(1.0) - 2.3025851 * jax.random.uniform(arg_keys[8], (D, Q), jnp.float32) ** shard_levels(arg_keys[8], (D, Q), ((0, 4), (1, 8)), -0.2, 0.2)), 0.1, 1.0),
        "noise_draw": centred(arg_keys[9], (D, Q), 1.0, 6.0, ((0, 4), (1, 8)), jnp.float32),
    }


beta_first = 0.9
beta_second = 0.99
beta_public = 0.9
public_epsilon = 0.001
adam_epsilon = 1e-08
clip_factor = 0.6
noise_level = 4.0
learn_rate = 0.01

def reference(public_tokens, public_targets, private_tokens, private_targets, token_counts, weight, public_moment, adam_first, adam_second, noise_draw):
    contract = (((0,), (0,)), ((), ()))
    w_half = weight.astype(jnp.bfloat16)
    public_out = jnp.dot(public_tokens, w_half, preferred_element_type=jnp.float32)
    public_delta = (public_out - public_targets.astype(jnp.float32)).astype(jnp.bfloat16)
    public_grad = lax.dot_general(public_tokens, public_delta, contract, preferred_element_type=jnp.float32) / math.sqrt(PUB)
    new_public = beta_public * public_moment + (1.0 - beta_public) * public_grad * public_grad
    precond = 1.0 / (jnp.sqrt(new_public) + public_epsilon)
    private_out = jnp.dot(private_tokens, w_half, preferred_element_type=jnp.float32)
    row_index = jnp.arange(PRIV, dtype=jnp.int32)
    owners = (row_index // L).astype(jnp.int32)
    limits = token_counts.reshape(-1)[owners]
    valid = row_index % L < limits
    private_delta = jnp.where(valid[:, None], private_out - private_targets.astype(jnp.float32), 0.0).astype(jnp.bfloat16)

    def example_norm(example):
        first_row = (example * L).astype(jnp.int32)
        block_x = lax.dynamic_slice_in_dim(private_tokens, first_row, L, 0)
        block_d = lax.dynamic_slice_in_dim(private_delta, first_row, L, 0)
        grads = lax.dot_general(block_x, block_d, contract, preferred_element_type=jnp.float32)
        scaled = grads * precond
        return jnp.sum(scaled * scaled)
    squares = lax.map(example_norm, jnp.arange(EXAMPLES, dtype=jnp.int32))
    clip_norm = clip_factor * math.sqrt(L * D * Q)
    factors = clip_norm / jnp.maximum(jnp.sqrt(squares), clip_norm)
    weighted = (factors[owners][:, None] * private_delta.astype(jnp.float32)).astype(jnp.bfloat16)
    summed = precond * lax.dot_general(private_tokens, weighted, contract, preferred_element_type=jnp.float32)
    noise_scale = noise_level * clip_factor * math.sqrt(L)
    gradient = (summed + noise_scale * noise_draw) / EXAMPLES
    new_first = beta_first * adam_first + (1.0 - beta_first) * gradient
    new_second = beta_second * adam_second + (1.0 - beta_second) * gradient * gradient
    first_hat = new_first / (1.0 - beta_first ** 2)
    second_hat = new_second / (1.0 - beta_second ** 2)
    new_weight = weight - learn_rate * first_hat / (jnp.sqrt(second_hat) + adam_epsilon)
    return (new_weight, new_first, new_second, new_public)
```

```python
import math

import jax
import jax.numpy as jnp
from jax import lax
from jax.experimental import pallas as pl
from jax.experimental.pallas import tpu as pltpu
from jax.sharding import PartitionSpec as P

beta_first = 0.9
beta_second = 0.99
beta_public = 0.9
public_epsilon = 0.001
adam_epsilon = 1e-08
clip_factor = 0.6
noise_level = 4.0
learn_rate = 0.01
contract_rows = (((0,), (0,)), ((), ()))


def swap(value, bit):
    size = lax.axis_size("tile")
    return lax.ppermute(value, "tile", [(i, i ^ bit) for i in range(size)])


def bits_of(size, backwards):
    order = [1 << k for k in range(size.bit_length() - 1)]
    return order[::-1] if backwards else order


def sum_to_owner(value, backwards):
    size = lax.axis_size("tile")
    me = lax.axis_index("tile")
    groups, _, rows, cols = value.shape
    order = bits_of(size, backwards)
    names = [1 << k for k in range(size.bit_length() - 1)][::-1]
    value = value.reshape((groups,) + (2,) * len(names) + (rows, cols))
    for bit in order:
        axis = 1 + names.index(bit)
        names.remove(bit)
        mine = (me // bit) % 2
        away = lax.dynamic_index_in_dim(value, 1 - mine, axis, keepdims=False)
        kept = lax.dynamic_index_in_dim(value, mine, axis, keepdims=False)
        value = kept + swap(away.astype(jnp.bfloat16), bit).astype(jnp.float32)
    return value


def gather_tiles(value, backwards):
    size = lax.axis_size("tile")
    me = lax.axis_index("tile")
    groups, rows, cols = value.shape
    names = []
    for bit in bits_of(size, backwards):
        mine = (me // bit) % 2
        other = swap(value, bit)
        names = sorted(names + [bit], reverse=True)
        axis = 1 + names.index(bit)
        low = jnp.where(mine == 0, value, other)
        high = jnp.where(mine == 0, other, value)
        value = jnp.stack([low, high], axis=axis)
    return value.reshape(groups, size, rows, cols)


def norm_kernel(x_ref, d_ref, p_ref, out_ref):
    total = jnp.zeros(out_ref.shape[1:], jnp.float32)
    rows = x_ref.shape[1]
    step = 256 if rows % 256 == 0 else 64
    for at in range(0, rows, step):
        grads = lax.dot_general(
            x_ref[:, at : at + step], d_ref[...], contract_rows, preferred_element_type=jnp.float32
        )
        scaled = grads * p_ref[at : at + step, :]
        total += jnp.sum((scaled * scaled).reshape(step // 8, 8, -1), axis=0)
    out_ref[0] = total


def example_squares(tokens, delta, precond, examples):
    slots, rows = tokens.shape
    seq_len = slots // examples
    cols = delta.shape[1]
    parts = pl.pallas_call(
        norm_kernel,
        grid=(examples,),
        in_specs=[
            pl.BlockSpec((seq_len, rows), lambda j: (j, 0)),
            pl.BlockSpec((seq_len, cols), lambda j: (j, 0)),
            pl.BlockSpec((rows, cols), lambda j: (0, 0)),
        ],
        out_specs=pl.BlockSpec((1, 8, cols), lambda j: (j, 0, 0)),
        out_shape=jax.ShapeDtypeStruct((examples, 8, cols), jnp.float32),
        compiler_params=pltpu.CompilerParams(vmem_limit_bytes=40 * 1024 * 1024),
        cost_estimate=pl.CostEstimate(
            flops=2 * slots * rows * cols, bytes_accessed=2 * slots * (rows + cols), transcendentals=0
        ),
        name="example_norms",
    )(tokens, delta, precond)
    return jnp.sum(parts, axis=(1, 2))


def errors_of(tokens, weight, targets, replicas, pieces):
    size = lax.axis_size("tile")
    cols = weight.shape[1]
    span = tokens.shape[0] // replicas
    per = replicas // pieces
    found = []
    for piece in range(pieces):
        block = tokens[piece * per * span : (piece + 1) * per * span]
        out = jnp.dot(block, weight, preferred_element_type=jnp.float32)
        out = sum_to_owner(out.reshape(per, size, span // size, cols), piece % 2 == 1)
        aims = targets[piece * per : (piece + 1) * per].astype(jnp.float32)
        delta = (out - aims).astype(jnp.bfloat16)
        found.append(gather_tiles(delta, piece % 2 == 1).reshape(per * span, cols))
    return jnp.concatenate(found, axis=0)


def on_device(
    public_tokens,
    public_targets,
    private_tokens,
    private_targets,
    token_counts,
    weight,
    public_moment,
    adam_first,
    adam_second,
    noise_draw,
):
    replicas = lax.axis_size("replica")
    tiles = lax.axis_size("tile")
    replica = lax.axis_index("replica")
    examples_here = token_counts.shape[1]
    examples_total = examples_here * replicas
    slots_here = private_tokens.shape[0]
    seq_len = slots_here // examples_here
    width = weight.shape[0] * tiles
    columns = weight.shape[1] * replicas
    cols = weight.shape[1]
    public_total = public_tokens.shape[0] * replicas

    limits = jnp.repeat(token_counts[0], seq_len, total_repeat_length=slots_here)
    live = jnp.arange(slots_here, dtype=jnp.int32) % seq_len < limits
    private_tokens = jnp.where(live[:, None], private_tokens, jnp.zeros((), private_tokens.dtype))

    w_half = weight.astype(jnp.bfloat16)
    aims = jnp.concatenate([public_targets, private_targets], axis=0)
    aims = lax.all_to_all(aims, "replica", split_axis=1, concat_axis=0, tiled=True)
    aims = aims.reshape(replicas, -1, cols)
    public_aims = aims[:, : public_targets.shape[0]]
    private_aims = aims[:, public_targets.shape[0] :]

    public_all = lax.all_gather(public_tokens, "replica", axis=0, tiled=True)
    private_all = lax.all_gather(private_tokens, "replica", axis=0, tiled=True)

    public_delta = errors_of(public_all, w_half, public_aims, replicas, 2)
    public_grad = lax.dot_general(
        public_all, public_delta, contract_rows, preferred_element_type=jnp.float32
    ) / math.sqrt(public_total)
    new_public = beta_public * public_moment + (1.0 - beta_public) * public_grad * public_grad
    precond = 1.0 / (jnp.sqrt(new_public) + public_epsilon)

    private_delta = errors_of(private_all, w_half, private_aims, replicas, 2)
    squares = example_squares(private_all, private_delta, precond, examples_total)
    squares = lax.psum(squares, ("replica", "tile"))
    clip_norm = clip_factor * math.sqrt(seq_len * width * columns)
    factors = clip_norm / jnp.maximum(jnp.sqrt(squares), clip_norm)
    slot_factor = jnp.repeat(factors, seq_len, total_repeat_length=slots_here * replicas)
    weighted = (slot_factor[:, None] * private_delta.astype(jnp.float32)).astype(jnp.bfloat16)
    summed = precond * lax.dot_general(
        private_all, weighted, contract_rows, preferred_element_type=jnp.float32
    )
    noise_scale = noise_level * clip_factor * math.sqrt(seq_len)
    gradient = (summed + noise_scale * noise_draw) / examples_total
    new_first = beta_first * adam_first + (1.0 - beta_first) * gradient
    new_second = beta_second * adam_second + (1.0 - beta_second) * gradient * gradient
    first_hat = new_first / (1.0 - beta_first**2)
    second_hat = new_second / (1.0 - beta_second**2)
    new_weight = weight - learn_rate * first_hat / (jnp.sqrt(second_hat) + adam_epsilon)
    return (new_weight, new_first, new_second, new_public)


def solution(mesh):
    placed = (
        P("replica", "tile"),
        P(("replica", "tile"), None),
        P("replica", "tile"),
        P(("replica", "tile"), None),
        P("replica", None),
        P("tile", "replica"),
        P("tile", "replica"),
        P("tile", "replica"),
        P("tile", "replica"),
        P("tile", "replica"),
    )
    return jax.shard_map(
        on_device,
        mesh=mesh,
        in_specs=placed,
        out_specs=(
            P("tile", "replica"),
            P("tile", "replica"),
            P("tile", "replica"),
            P("tile", "replica"),
        ),
        check_vma=False,
    )
```

```python
import functools
import math

import jax
import jax.numpy as jnp
from jax import lax
from jax.experimental import pallas as pl
from jax.experimental.pallas import tpu as pltpu
from jax.sharding import PartitionSpec as P

beta_first = 0.9
beta_second = 0.99
beta_public = 0.9
public_epsilon = 0.001
adam_epsilon = 1e-08
clip_factor = 0.6
noise_level = 4.0
learn_rate = 0.01
contract_rows = (((0,), (0,)), ((), ()))


MESH = pl.DeviceIdType.MESH
CORES = 2


def errors_kernel(
    pub_x, prv_x, pub_t, prv_t, w_ref,
    pub_all, prv_all, pub_d, prv_d,
    pub_aims, prv_aims, pub_send, prv_send, pub_recv, prv_recv, pub_own, prv_own, pub_y, prv_y,
    x_recv, up_sem, down_sem, core_sem, aim_recv, aim_sent, rs_recv, rs_sent, ag_recv, ag_sent,
):
    replicas = lax.axis_size("replica")
    tiles = lax.axis_size("tile")
    r = lax.axis_index("replica")
    t = lax.axis_index("tile")
    chips = replicas // CORES
    z = r // CORES
    c = r % CORES
    cols = w_ref.shape[1]
    inner = jnp.minimum(z, chips - 1 - z)
    phases = (
        (pub_x, pub_t, pub_all, pub_d, pub_aims, pub_send, pub_recv, pub_own, pub_y),
        (prv_x, prv_t, prv_all, prv_d, prv_aims, prv_send, prv_recv, prv_own, prv_y),
    )

    def to(src, dst, sent, got, replica, tile):
        return pltpu.make_async_remote_copy(
            src_ref=src, dst_ref=dst, send_sem=sent, recv_sem=got,
            device_id=(replica, tile), device_id_type=MESH,
        )

    def chip_at(i):
        k = (i + 1) // 2
        paired = jnp.where(i % 2 == 1, z - k, z + k)
        rest = jnp.where(z < chips - 1 - z, z + (i - inner), z - (i - inner))
        return jnp.where(i <= 2 * inner, paired, rest)

    def token_copy(f, q, sent, replica):
        ref = phases[f][2].at[q]
        return to(ref, ref, sent, x_recv.at[f, q], replica, t)

    def aim_copy(f, d):
        other = (r + d) % replicas
        ref = phases[f][1].at[:, pl.ds(pl.multiple_of(other * cols, cols), cols)]
        return to(ref, phases[f][4].at[d - 1], aim_sent.at[f, d - 1], aim_recv.at[f, d - 1], other, t)

    def part_copy(f, q, d):
        there = (t + d) % tiles
        return to(
            phases[f][5].at[q, there], phases[f][6].at[q, d - 1],
            rs_sent.at[f, q, d - 1], rs_recv.at[f, q, d - 1], r, there,
        )

    def error_copy(f, q, d):
        there = (t + d) % tiles
        ref = phases[f][3].at[q, t]
        return to(ref, ref, ag_sent.at[f, q, d - 1], ag_recv.at[f, q, d - 1], r, there)

    def error_arrival(f, q, d):
        ref = phases[f][3].at[q, (t + tiles - d) % tiles]
        return to(ref, ref, ag_sent.at[f, q, d - 1], ag_recv.at[f, q, d - 1], r, (t + tiles - d) % tiles)

    barrier = pltpu.get_barrier_semaphore()
    for d in range(1, replicas):
        pl.semaphore_signal(barrier, inc=1, device_id=((r + d) % replicas, t), device_id_type=MESH)
    for d in range(1, tiles):
        pl.semaphore_signal(barrier, inc=1, device_id=(r, (t + d) % tiles), device_id_type=MESH)
    pub_all[r] = pub_x[...]
    prv_all[r] = prv_x[...]
    pl.semaphore_wait(barrier, replicas + tiles - 2)

    def along(f, i, chip):
        mine = chip * CORES + c

        @pl.when(jnp.logical_and(chip <= z, z < chips - 1))
        def _():
            token_copy(f, mine, up_sem.at[f, i], r + CORES).start()

        @pl.when(jnp.logical_and(chip >= z, z > 0))
        def _():
            token_copy(f, mine, down_sem.at[f, i], r - CORES).start()

    def along_done(f, i):
        chip = chip_at(i)
        mine = chip * CORES + c

        @pl.when(jnp.logical_and(chip <= z, z < chips - 1))
        def _():
            token_copy(f, mine, up_sem.at[f, i], r + CORES).wait_send()

        @pl.when(jnp.logical_and(chip >= z, z > 0))
        def _():
            token_copy(f, mine, down_sem.at[f, i], r - CORES).wait_send()

    def partial(f, q):
        x_all, send, own, y = phases[f][2], phases[f][5], phases[f][7], phases[f][8]
        sub = y.shape[1]
        out = jnp.dot(x_all[q], w_ref[...], preferred_element_type=jnp.float32)
        for at in range(tiles):
            part = out[at * sub : (at + 1) * sub]
            y[at] = part
            send[q, at] = part.astype(jnp.bfloat16)
        for d in range(1, tiles):
            part_copy(f, q, d).start()
        own[q] = y[t]

    def finish(f, q):
        d_all, aims, recv, own = phases[f][3], phases[f][4], phases[f][6], phases[f][7]
        gap = (r + replicas - q) % replicas

        @pl.when(gap > 0)
        def _():
            to(aims.at[gap - 1], aims.at[gap - 1], aim_sent.at[f, gap - 1], aim_recv.at[f, gap - 1], q, t).wait_recv()
            own[q] = own[q] - aims[gap - 1].astype(jnp.float32)

        @pl.when(gap == 0)
        def _():
            mine = phases[f][1][:, pl.ds(pl.multiple_of(r * cols, cols), cols)]
            own[q] = own[q] - mine.astype(jnp.float32)

        total = own[q]
        for d in range(1, tiles):
            part_copy(f, q, d).wait_recv()
            total = total + recv[q, d - 1].astype(jnp.float32)
        d_all[q, t] = total.astype(jnp.bfloat16)
        for d in range(1, tiles):
            error_copy(f, q, d).start()

    def phase(f):
        def body(i, carry):
            @pl.when(i < chips)
            def _():
                chip = chip_at(i)
                mine = chip * CORES + c
                other = chip * CORES + 1 - c

                @pl.when(i > 0)
                def _():
                    token_copy(f, mine, up_sem.at[f, i], r).wait_recv()

                if f == 0:
                    along(f, i, chip)
                else:
                    @pl.when(i > 0)
                    def _():
                        along(f, i, chip)
                token_copy(f, mine, core_sem.at[f, i], z * CORES + 1 - c).start()

                @pl.when(i == 0)
                def _():
                    for d in range(1, replicas):
                        aim_copy(f, d).start()

                if f == 0:
                    @pl.when(i == min(1, chips - 1))
                    def _():
                        along(1, 0, z)

                partial(f, mine)
                token_copy(f, other, core_sem.at[f, i], r).wait_recv()
                partial(f, other)

            @pl.when(i > 0)
            def _():
                chip = chip_at(i - 1)
                finish(f, chip * CORES + c)
                finish(f, chip * CORES + 1 - c)

            return carry

        lax.fori_loop(0, chips + 1, body, 0)

    phase(0)
    phase(1)

    def close(f):
        def body(q, carry):
            for d in range(1, tiles):
                error_arrival(f, q, d).wait_recv()
                error_copy(f, q, d).wait_send()
                part_copy(f, q, d).wait_send()
            return carry

        lax.fori_loop(0, replicas, body, 0)

        def sent(i, carry):
            along_done(f, i)
            token_copy(f, chip_at(i) * CORES + c, core_sem.at[f, i], r).wait_send()
            return carry

        lax.fori_loop(0, chips, sent, 0)
        for d in range(1, replicas):
            aim_copy(f, d).wait_send()

    close(0)
    close(1)


def gathered_errors(pub_x, prv_x, pub_t, prv_t, w_half):
    replicas = lax.axis_size("replica")
    tiles = lax.axis_size("tile")
    chips = replicas // CORES
    rows, cols = w_half.shape
    half, full = jnp.bfloat16, jnp.float32
    spans = (pub_x.shape[0], prv_x.shape[0])
    subs = [span // tiles for span in spans]
    vmem = pl.BlockSpec(memory_space=pltpu.VMEM)
    scratch = [pltpu.VMEM((replicas - 1, sub, cols), half) for sub in subs]
    scratch += [pltpu.VMEM((replicas, tiles, sub, cols), half) for sub in subs]
    scratch += [pltpu.VMEM((replicas, tiles - 1, sub, cols), half) for sub in subs]
    scratch += [pltpu.VMEM((replicas, sub, cols), full) for sub in subs]
    scratch += [pltpu.VMEM((tiles, sub, cols), full) for sub in subs]
    sems = [(2, replicas), (2, chips), (2, chips), (2, chips), (2, replicas - 1), (2, replicas - 1)]
    sems += [(2, replicas, tiles - 1)] * 4
    scratch += [pltpu.SemaphoreType.DMA(shape) for shape in sems]
    flops = 2 * replicas * sum(spans) * rows * cols
    return pl.pallas_call(
        errors_kernel,
        out_shape=[jax.ShapeDtypeStruct((replicas, span, rows), half) for span in spans]
        + [jax.ShapeDtypeStruct((replicas, tiles, sub, cols), half) for sub in subs],
        in_specs=[vmem] * 5,
        out_specs=[vmem] * 4,
        scratch_shapes=scratch,
        compiler_params=pltpu.CompilerParams(
            collective_id=0, has_side_effects=True, vmem_limit_bytes=56 * 1024 * 1024
        ),
        cost_estimate=pl.CostEstimate(flops=flops, bytes_accessed=2 * replicas * sum(spans) * rows, transcendentals=0),
        name="gathered_errors",
    )(pub_x, prv_x, pub_t, prv_t, w_half)


def norm_kernel(x_ref, d_ref, p_ref, out_ref):
    total = jnp.zeros(out_ref.shape[1:], jnp.float32)
    rows = x_ref.shape[1]
    step = 256 if rows % 256 == 0 else 64
    for at in range(0, rows, step):
        grads = lax.dot_general(
            x_ref[:, at : at + step], d_ref[...], contract_rows, preferred_element_type=jnp.float32
        )
        scaled = grads * p_ref[at : at + step, :]
        total += jnp.sum((scaled * scaled).reshape(step // 8, 8, -1), axis=0)
    out_ref[0] = total


def example_squares(tokens, delta, precond, examples):
    slots, rows = tokens.shape
    seq_len = slots // examples
    cols = delta.shape[1]
    parts = pl.pallas_call(
        norm_kernel,
        grid=(examples,),
        in_specs=[
            pl.BlockSpec((seq_len, rows), lambda j: (j, 0)),
            pl.BlockSpec((seq_len, cols), lambda j: (j, 0)),
            pl.BlockSpec((rows, cols), lambda j: (0, 0)),
        ],
        out_specs=pl.BlockSpec((1, 8, cols), lambda j: (j, 0, 0)),
        out_shape=jax.ShapeDtypeStruct((examples, 8, cols), jnp.float32),
        compiler_params=pltpu.CompilerParams(vmem_limit_bytes=40 * 1024 * 1024),
        cost_estimate=pl.CostEstimate(
            flops=2 * slots * rows * cols, bytes_accessed=2 * slots * (rows + cols), transcendentals=0
        ),
        name="example_norms",
    )(tokens, delta, precond)
    return jnp.sum(parts, axis=(1, 2))


def update_kernel(
    total_examples, noise_scale, f_ref, x_ref, d_ref, p_ref, n_ref, m_ref, v_ref, w_ref,
    new_w, new_m, new_v, weighted,
):
    examples = f_ref.shape[0]
    seq_len = d_ref.shape[0] // examples

    @pl.when(pl.program_id(0) == 0)
    def _():
        for j in range(examples):
            at = slice(j * seq_len, (j + 1) * seq_len)
            weighted[at, :] = (f_ref[j] * d_ref[at, :].astype(jnp.float32)).astype(jnp.bfloat16)

    summed = p_ref[...] * lax.dot_general(
        x_ref[...], weighted[...], contract_rows, preferred_element_type=jnp.float32
    )
    gradient = (summed + noise_scale * n_ref[...]) * (1.0 / total_examples)
    first = beta_first * m_ref[...] + (1.0 - beta_first) * gradient
    second = beta_second * v_ref[...] + (1.0 - beta_second) * gradient * gradient
    new_m[...] = first
    new_v[...] = second
    first_hat = first * (1.0 / (1.0 - beta_first**2))
    second_hat = second * (1.0 / (1.0 - beta_second**2))
    new_w[...] = w_ref[...] - learn_rate * first_hat / (jnp.sqrt(second_hat) + adam_epsilon)


def update(factors, tokens, delta, precond, noise, first, second, weight, noise_scale):
    slots, rows = tokens.shape
    cols = delta.shape[1]
    examples = factors.shape[0]
    step = 256 if rows % 256 == 0 else rows
    state = pl.BlockSpec((step, cols), lambda i: (i, 0))
    return pl.pallas_call(
        functools.partial(update_kernel, examples, noise_scale),
        grid=(rows // step,),
        in_specs=[
            pl.BlockSpec(memory_space=pltpu.SMEM),
            pl.BlockSpec((slots, step), lambda i: (0, i)),
            pl.BlockSpec((slots, cols), lambda i: (0, 0)),
        ]
        + [state] * 5,
        out_specs=[state] * 3,
        out_shape=[jax.ShapeDtypeStruct((rows, cols), jnp.float32)] * 3,
        scratch_shapes=[pltpu.VMEM((slots, cols), jnp.bfloat16)],
        compiler_params=pltpu.CompilerParams(vmem_limit_bytes=48 * 1024 * 1024),
        cost_estimate=pl.CostEstimate(
            flops=2 * slots * rows * cols,
            bytes_accessed=2 * slots * (rows + cols) + 32 * rows * cols,
            transcendentals=rows * cols,
        ),
        name="update",
    )(factors, tokens, delta, precond, noise, first, second, weight)


def on_device(
    public_tokens,
    public_targets,
    private_tokens,
    private_targets,
    token_counts,
    weight,
    public_moment,
    adam_first,
    adam_second,
    noise_draw,
):
    replicas = lax.axis_size("replica")
    tiles = lax.axis_size("tile")
    examples_here = token_counts.shape[1]
    examples_total = examples_here * replicas
    slots_here = private_tokens.shape[0]
    seq_len = slots_here // examples_here
    width = weight.shape[0] * tiles
    columns = weight.shape[1] * replicas
    cols = weight.shape[1]
    public_total = public_tokens.shape[0] * replicas

    limits = jnp.repeat(token_counts[0], seq_len, total_repeat_length=slots_here)
    live = jnp.arange(slots_here, dtype=jnp.int32) % seq_len < limits
    private_tokens = jnp.where(live[:, None], private_tokens, jnp.zeros((), private_tokens.dtype))

    w_half = weight.astype(jnp.bfloat16)
    public_all, private_all, public_delta, private_delta = gathered_errors(
        public_tokens, private_tokens, public_targets, private_targets, w_half
    )
    public_all = public_all.reshape(public_total, -1)
    public_delta = public_delta.reshape(public_total, cols)
    private_all = private_all.reshape(slots_here * replicas, -1)
    private_delta = private_delta.reshape(slots_here * replicas, cols)

    public_grad = lax.dot_general(
        public_all, public_delta, contract_rows, preferred_element_type=jnp.float32
    ) / math.sqrt(public_total)
    new_public = beta_public * public_moment + (1.0 - beta_public) * public_grad * public_grad
    precond = 1.0 / (jnp.sqrt(new_public) + public_epsilon)

    squares = example_squares(private_all, private_delta, precond, examples_total)
    squares = lax.psum(squares, ("replica", "tile"))
    clip_norm = clip_factor * math.sqrt(seq_len * width * columns)
    factors = clip_norm / jnp.maximum(jnp.sqrt(squares), clip_norm)
    noise_scale = noise_level * clip_factor * math.sqrt(seq_len)
    new_weight, new_first, new_second = update(
        factors, private_all, private_delta, precond, noise_draw, adam_first, adam_second, weight, noise_scale
    )
    return (new_weight, new_first, new_second, new_public)


def solution(mesh):
    placed = (
        P("replica", "tile"),
        P(("replica", "tile"), None),
        P("replica", "tile"),
        P(("replica", "tile"), None),
        P("replica", None),
        P("tile", "replica"),
        P("tile", "replica"),
        P("tile", "replica"),
        P("tile", "replica"),
        P("tile", "replica"),
    )
    return jax.shard_map(
        on_device,
        mesh=mesh,
        in_specs=placed,
        out_specs=(
            P("tile", "replica"),
            P("tile", "replica"),
            P("tile", "replica"),
            P("tile", "replica"),
        ),
        check_vma=False,
    )
```

```python
import functools
import math

import jax
import jax.numpy as jnp
from jax import lax
from jax.experimental import pallas as pl
from jax.experimental.pallas import tpu as pltpu
from jax.sharding import PartitionSpec as P

beta_first = 0.9
beta_second = 0.99
beta_public = 0.9
public_epsilon = 0.001
adam_epsilon = 1e-08
clip_factor = 0.6
noise_level = 4.0
learn_rate = 0.01
contract_rows = (((0,), (0,)), ((), ()))


MESH = pl.DeviceIdType.MESH
CORES = 2


def errors_kernel(
    root, clip_norm,
    pub_x, prv_x, pub_t, prv_t, counts, weight, moment,
    prv_all, prv_d, new_public, precond, factors,
    pub_all, pub_d, w_ref, squares, tile_squares, all_squares,
    pub_aims, prv_aims, pub_send, prv_send, pub_recv, prv_recv, pub_own, prv_own, pub_y, prv_y,
    x_recv, up_sem, down_sem, core_sem, aim_recv, aim_sent, rs_recv, rs_sent, ag_recv, ag_sent,
    tile_recv, tile_sent, all_recv, all_sent,
):
    replicas = lax.axis_size("replica")
    tiles = lax.axis_size("tile")
    r = lax.axis_index("replica")
    t = lax.axis_index("tile")
    chips = replicas // CORES
    z = r // CORES
    c = r % CORES
    cols = w_ref.shape[1]
    inner = jnp.minimum(z, chips - 1 - z)
    phases = (
        (pub_x, pub_t, pub_all, pub_d, pub_aims, pub_send, pub_recv, pub_own, pub_y),
        (prv_x, prv_t, prv_all, prv_d, prv_aims, prv_send, prv_recv, prv_own, prv_y),
    )

    def to(src, dst, sent, got, replica, tile):
        return pltpu.make_async_remote_copy(
            src_ref=src, dst_ref=dst, send_sem=sent, recv_sem=got,
            device_id=(replica, tile), device_id_type=MESH,
        )

    def chip_at(i):
        k = (i + 1) // 2
        longer = jnp.where(z < chips - 1 - z, 1, -1)
        paired = jnp.where(i % 2 == 1, z + longer * k, z - longer * k)
        rest = z + longer * (i - inner)
        return jnp.where(i <= 2 * inner, paired, rest)

    def token_copy(f, q, sent, replica):
        ref = phases[f][2].at[q]
        return to(ref, ref, sent, x_recv.at[f, q], replica, t)

    def aim_copy(f, d):
        other = (r + d) % replicas
        ref = phases[f][1].at[:, pl.ds(pl.multiple_of(other * cols, cols), cols)]
        return to(ref, phases[f][4].at[d - 1], aim_sent.at[f, d - 1], aim_recv.at[f, d - 1], other, t)

    def part_copy(f, q, d):
        there = (t + d) % tiles
        return to(
            phases[f][5].at[q, there], phases[f][6].at[q, d - 1],
            rs_sent.at[f, q, d - 1], rs_recv.at[f, q, d - 1], r, there,
        )

    def error_copy(f, q, d):
        there = (t + d) % tiles
        ref = phases[f][3].at[q, t]
        return to(ref, ref, ag_sent.at[f, q, d - 1], ag_recv.at[f, q, d - 1], r, there)

    def error_arrival(f, q, d):
        ref = phases[f][3].at[q, (t + tiles - d) % tiles]
        return to(ref, ref, ag_sent.at[f, q, d - 1], ag_recv.at[f, q, d - 1], r, (t + tiles - d) % tiles)

    barrier = pltpu.get_barrier_semaphore()
    for d in range(1, replicas):
        pl.semaphore_signal(barrier, inc=1, device_id=((r + d) % replicas, t), device_id_type=MESH)
    for d in range(1, tiles):
        pl.semaphore_signal(barrier, inc=1, device_id=(r, (t + d) % tiles), device_id_type=MESH)
    pub_all[r] = pub_x[...]
    examples = counts.shape[1]
    seq_len = prv_x.shape[0] // examples
    row = lax.broadcasted_iota(jnp.int32, (seq_len, 1), 0)
    for e in range(examples):
        live = (row < counts[0, e]).astype(jnp.float32)
        at = slice(e * seq_len, (e + 1) * seq_len)
        prv_all[r, at, :] = (prv_x[at, :].astype(jnp.float32) * live).astype(jnp.bfloat16)
    w_ref[...] = weight[...].astype(jnp.bfloat16)
    pl.semaphore_wait(barrier, replicas + tiles - 2)

    def along(f, i, chip):
        mine = chip * CORES + c

        @pl.when(jnp.logical_and(chip <= z, z < chips - 1))
        def _():
            token_copy(f, mine, up_sem.at[f, i], r + CORES).start()

        @pl.when(jnp.logical_and(chip >= z, z > 0))
        def _():
            token_copy(f, mine, down_sem.at[f, i], r - CORES).start()

    def along_done(f, i):
        chip = chip_at(i)
        mine = chip * CORES + c

        @pl.when(jnp.logical_and(chip <= z, z < chips - 1))
        def _():
            token_copy(f, mine, up_sem.at[f, i], r + CORES).wait_send()

        @pl.when(jnp.logical_and(chip >= z, z > 0))
        def _():
            token_copy(f, mine, down_sem.at[f, i], r - CORES).wait_send()

    def partial(f, q):
        x_all, send, own, y = phases[f][2], phases[f][5], phases[f][7], phases[f][8]
        sub = y.shape[1]
        out = jnp.dot(x_all[q], w_ref[...], preferred_element_type=jnp.float32)
        for at in range(tiles):
            part = out[at * sub : (at + 1) * sub]
            y[at] = part
            send[q, at] = part.astype(jnp.bfloat16)
        for d in range(1, tiles):
            part_copy(f, q, d).start()
        own[q] = y[t]

    def finish(f, q):
        d_all, aims, recv, own = phases[f][3], phases[f][4], phases[f][6], phases[f][7]
        gap = (r + replicas - q) % replicas

        @pl.when(gap > 0)
        def _():
            to(aims.at[gap - 1], aims.at[gap - 1], aim_sent.at[f, gap - 1], aim_recv.at[f, gap - 1], q, t).wait_recv()
            own[q] = own[q] - aims[gap - 1].astype(jnp.float32)

        @pl.when(gap == 0)
        def _():
            mine = phases[f][1][:, pl.ds(pl.multiple_of(r * cols, cols), cols)]
            own[q] = own[q] - mine.astype(jnp.float32)

        total = own[q]
        for d in range(1, tiles):
            part_copy(f, q, d).wait_recv()
            total = total + recv[q, d - 1].astype(jnp.float32)
        d_all[q, t] = total.astype(jnp.bfloat16)
        for d in range(1, tiles):
            error_copy(f, q, d).start()

    def arrived(f, q):
        for d in range(1, tiles):
            error_arrival(f, q, d).wait_recv()

    rows = weight.shape[0]
    step = 256 if rows % 256 == 0 else rows

    def public_update():
        def waiting(q, carry):
            arrived(0, q)
            return carry

        lax.fori_loop(0, replicas, waiting, 0)
        total = replicas * pub_x.shape[0]
        errors = pub_d[...].reshape(total, cols)
        for at in range(0, rows, step):
            tokens = pub_all[:, :, at : at + step].reshape(total, step)
            grads = lax.dot_general(tokens, errors, contract_rows, preferred_element_type=jnp.float32)
            grads = grads * (1.0 / root)
            moved = beta_public * moment[at : at + step, :] + (1.0 - beta_public) * grads * grads
            new_public[at : at + step, :] = moved
            precond[at : at + step, :] = 1.0 / (jnp.sqrt(moved) + public_epsilon)

    def norms(chip):
        def body(which, carry):
            q = chip * CORES + (c + which) % CORES
            arrived(1, q)
            parts = [prv_d[q, at] for at in range(tiles)]
            if parts[0].shape[0] % 16 == 0:
                errors = jnp.concatenate(parts, axis=0)
            else:
                errors = jnp.concatenate([part.astype(jnp.float32) for part in parts], axis=0)
                errors = errors.astype(jnp.bfloat16)
            for e in range(examples):
                span = slice(e * seq_len, (e + 1) * seq_len)
                total = jnp.zeros((8, cols), jnp.float32)
                for at in range(0, rows, step):
                    grads = lax.dot_general(
                        prv_all[q, span, at : at + step], errors[span],
                        contract_rows, preferred_element_type=jnp.float32,
                    )
                    scaled = grads * precond[at : at + step, :]
                    total += jnp.sum((scaled * scaled).reshape(step // 8, 8, cols), axis=0)
                line = jnp.sum(total, axis=0, keepdims=True)
                line = sum(line[:, at : at + 128] for at in range(0, cols, 128))
                squares[pl.ds(q * examples + e, 1), :] = line
            return carry

        lax.fori_loop(0, CORES, body, 0)

    def tile_copy(d):
        return to(squares, tile_squares.at[d - 1], tile_sent.at[d - 1], tile_recv.at[d - 1], r, (t + d) % tiles)

    def all_copy(d):
        return to(
            factors, all_squares.at[d - 1], all_sent.at[d - 1], all_recv.at[d - 1], (r + d) % replicas, t
        )

    def phase(f):
        def body(i, carry):
            @pl.when(i < chips)
            def _():
                chip = chip_at(i)
                mine = chip * CORES + c
                other = chip * CORES + 1 - c

                @pl.when(i > 0)
                def _():
                    token_copy(f, mine, up_sem.at[f, i], r).wait_recv()

                if f == 0:
                    along(f, i, chip)
                else:
                    @pl.when(i > 0)
                    def _():
                        along(f, i, chip)
                token_copy(f, mine, core_sem.at[f, i], z * CORES + 1 - c).start()

                @pl.when(i == 0)
                def _():
                    for d in range(1, replicas):
                        aim_copy(f, d).start()

                if f == 0:
                    @pl.when(i == min(1, chips - 1))
                    def _():
                        along(1, 0, z)

                partial(f, mine)
                token_copy(f, other, core_sem.at[f, i], r).wait_recv()
                partial(f, other)

            @pl.when(jnp.logical_and(i > 0, i <= chips))
            def _():
                chip = chip_at(i - 1)
                finish(f, chip * CORES + c)
                finish(f, chip * CORES + 1 - c)

            if f == 1:
                @pl.when(i == 1)
                def _():
                    public_update()

                @pl.when(i > 1)
                def _():
                    norms(chip_at(i - 2))

            return carry

        lax.fori_loop(0, chips + 1 + f, body, 0)

    phase(0)
    phase(1)

    for d in range(1, tiles):
        tile_copy(d).start()
    for d in range(1, tiles):
        tile_copy(d).wait_recv()
    total = squares[...]
    for d in range(1, tiles):
        total = total + tile_squares[d - 1]
    factors[...] = total
    for d in range(1, replicas):
        all_copy(d).start()
    for d in range(1, replicas):
        all_copy(d).wait()
    for d in range(1, replicas):
        total = total + all_squares[d - 1]
    total = jnp.sum(total, axis=1, keepdims=True)
    factor = clip_norm / jnp.maximum(jnp.sqrt(total), clip_norm)
    factors[...] = jnp.broadcast_to(factor, factors.shape)
    for d in range(1, tiles):
        tile_copy(d).wait_send()

    def close(f):
        def body(q, carry):
            for d in range(1, tiles):
                error_copy(f, q, d).wait_send()
                part_copy(f, q, d).wait_send()
            return carry

        lax.fori_loop(0, replicas, body, 0)

        def sent(i, carry):
            along_done(f, i)
            token_copy(f, chip_at(i) * CORES + c, core_sem.at[f, i], r).wait_send()
            return carry

        lax.fori_loop(0, chips, sent, 0)
        for d in range(1, replicas):
            aim_copy(f, d).wait_send()

    close(0)
    close(1)


def gathered_errors(pub_x, prv_x, pub_t, prv_t, counts, weight, moment, root, clip_norm):
    replicas = lax.axis_size("replica")
    tiles = lax.axis_size("tile")
    chips = replicas // CORES
    rows, cols = weight.shape
    half, full = jnp.bfloat16, jnp.float32
    spans = (pub_x.shape[0], prv_x.shape[0])
    subs = [span // tiles for span in spans]
    examples = counts.shape[1] * replicas
    vmem = pl.BlockSpec(memory_space=pltpu.VMEM)
    tokens = [(replicas, span, rows) for span in spans]
    errors = [(replicas, tiles, sub, cols) for sub in subs]
    scratch = [pltpu.VMEM(tokens[0], half), pltpu.VMEM(errors[0], half), pltpu.VMEM((rows, cols), half)]
    scratch += [pltpu.VMEM(shape + (examples, 128), full) for shape in ((), (tiles - 1,), (replicas - 1,))]
    scratch += [pltpu.VMEM((replicas - 1, sub, cols), half) for sub in subs]
    scratch += [pltpu.VMEM((replicas, tiles, sub, cols), half) for sub in subs]
    scratch += [pltpu.VMEM((replicas, tiles - 1, sub, cols), half) for sub in subs]
    scratch += [pltpu.VMEM((replicas, sub, cols), full) for sub in subs]
    scratch += [pltpu.VMEM((tiles, sub, cols), full) for sub in subs]
    sems = [(2, replicas), (2, chips), (2, chips), (2, chips), (2, replicas - 1), (2, replicas - 1)]
    sems += [(2, replicas, tiles - 1)] * 4
    sems += [(tiles - 1,)] * 2 + [(replicas - 1,)] * 2
    scratch += [pltpu.SemaphoreType.DMA(shape) for shape in sems]
    flops = 4 * replicas * sum(spans) * rows * cols
    state = jax.ShapeDtypeStruct((rows, cols), full)
    return pl.pallas_call(
        functools.partial(errors_kernel, root, clip_norm),
        out_shape=[
            jax.ShapeDtypeStruct(tokens[1], half),
            jax.ShapeDtypeStruct(errors[1], half),
            state,
            state,
            jax.ShapeDtypeStruct((examples, 128), full),
        ],
        in_specs=[vmem] * 4 + [pl.BlockSpec(memory_space=pltpu.SMEM)] + [vmem] * 2,
        out_specs=[vmem] * 5,
        scratch_shapes=scratch,
        compiler_params=pltpu.CompilerParams(
            collective_id=0, has_side_effects=True, vmem_limit_bytes=58 * 1024 * 1024
        ),
        cost_estimate=pl.CostEstimate(flops=flops, bytes_accessed=2 * replicas * sum(spans) * rows, transcendentals=0),
        name="gathered_errors",
    )(pub_x, prv_x, pub_t, prv_t, counts, weight, moment)


def update_kernel(
    total_examples, noise_scale, f_ref, x_ref, d_ref, p_ref, n_ref, m_ref, v_ref, w_ref,
    new_w, new_m, new_v, weighted,
):
    examples = f_ref.shape[0]
    seq_len = d_ref.shape[0] // examples

    @pl.when(pl.program_id(0) == 0)
    def _():
        for j in range(examples):
            at = slice(j * seq_len, (j + 1) * seq_len)
            weighted[at, :] = (f_ref[j : j + 1, :1] * d_ref[at, :].astype(jnp.float32)).astype(jnp.bfloat16)

    summed = p_ref[...] * lax.dot_general(
        x_ref[...], weighted[...], contract_rows, preferred_element_type=jnp.float32
    )
    gradient = (summed + noise_scale * n_ref[...]) * (1.0 / total_examples)
    first = beta_first * m_ref[...] + (1.0 - beta_first) * gradient
    second = beta_second * v_ref[...] + (1.0 - beta_second) * gradient * gradient
    new_m[...] = first
    new_v[...] = second
    first_hat = first * (1.0 / (1.0 - beta_first**2))
    second_hat = second * (1.0 / (1.0 - beta_second**2))
    new_w[...] = w_ref[...] - learn_rate * first_hat / (jnp.sqrt(second_hat) + adam_epsilon)


def update(factors, tokens, delta, precond, noise, first, second, weight, noise_scale):
    slots, rows = tokens.shape
    cols = delta.shape[1]
    examples = factors.shape[0]
    step = 256 if rows % 256 == 0 else rows
    state = pl.BlockSpec((step, cols), lambda i: (i, 0))
    return pl.pallas_call(
        functools.partial(update_kernel, examples, noise_scale),
        grid=(rows // step,),
        in_specs=[
            pl.BlockSpec((examples, 128), lambda i: (0, 0)),
            pl.BlockSpec((slots, step), lambda i: (0, i)),
            pl.BlockSpec((slots, cols), lambda i: (0, 0)),
        ]
        + [state] * 5,
        out_specs=[state] * 3,
        out_shape=[jax.ShapeDtypeStruct((rows, cols), jnp.float32)] * 3,
        scratch_shapes=[pltpu.VMEM((slots, cols), jnp.bfloat16)],
        compiler_params=pltpu.CompilerParams(vmem_limit_bytes=48 * 1024 * 1024),
        cost_estimate=pl.CostEstimate(
            flops=2 * slots * rows * cols,
            bytes_accessed=2 * slots * (rows + cols) + 32 * rows * cols,
            transcendentals=rows * cols,
        ),
        name="update",
    )(factors, tokens, delta, precond, noise, first, second, weight)


def on_device(
    public_tokens,
    public_targets,
    private_tokens,
    private_targets,
    token_counts,
    weight,
    public_moment,
    adam_first,
    adam_second,
    noise_draw,
):
    replicas = lax.axis_size("replica")
    tiles = lax.axis_size("tile")
    examples_here = token_counts.shape[1]
    slots_here = private_tokens.shape[0]
    seq_len = slots_here // examples_here
    width = weight.shape[0] * tiles
    columns = weight.shape[1] * replicas
    cols = weight.shape[1]
    public_total = public_tokens.shape[0] * replicas

    clip_norm = clip_factor * math.sqrt(seq_len * width * columns)
    private_all, private_delta, new_public, precond, factors = gathered_errors(
        public_tokens, private_tokens, public_targets, private_targets, token_counts, weight, public_moment,
        math.sqrt(public_total), clip_norm,
    )
    private_all = private_all.reshape(slots_here * replicas, -1)
    private_delta = private_delta.reshape(slots_here * replicas, cols)
    noise_scale = noise_level * clip_factor * math.sqrt(seq_len)
    new_weight, new_first, new_second = update(
        factors, private_all, private_delta, precond, noise_draw, adam_first, adam_second, weight, noise_scale
    )
    return (new_weight, new_first, new_second, new_public)


def solution(mesh):
    placed = (
        P("replica", "tile"),
        P(("replica", "tile"), None),
        P("replica", "tile"),
        P(("replica", "tile"), None),
        P("replica", None),
        P("tile", "replica"),
        P("tile", "replica"),
        P("tile", "replica"),
        P("tile", "replica"),
        P("tile", "replica"),
    )
    return jax.shard_map(
        on_device,
        mesh=mesh,
        in_specs=placed,
        out_specs=(
            P("tile", "replica"),
            P("tile", "replica"),
            P("tile", "replica"),
            P("tile", "replica"),
        ),
        check_vma=False,
    )
```

```python
import functools
import math

import jax
import jax.numpy as jnp
from jax import lax
from jax.experimental import pallas as pl
from jax.experimental.pallas import tpu as pltpu
from jax.sharding import PartitionSpec as P

beta_first = 0.9
beta_second = 0.99
beta_public = 0.9
public_epsilon = 0.001
adam_epsilon = 1e-08
clip_factor = 0.6
noise_level = 4.0
learn_rate = 0.01
contract_rows = (((0,), (0,)), ((), ()))


MESH = pl.DeviceIdType.MESH
CORES = 2


def pieces_of(public_rows, private_rows):
    cut = 3 if private_rows % 48 == 0 else 1
    private = private_rows // cut
    return [(0, 0, public_rows)] + [(1, at * private, private) for at in range(cut)]


def dense(parts):
    if parts[0].shape[0] % 16 == 0:
        return jnp.concatenate(parts, axis=0)
    return jnp.concatenate([part.astype(jnp.float32) for part in parts], axis=0).astype(parts[0].dtype)


def errors_kernel(
    root, clip_norm,
    pub_x, prv_x, pub_t, prv_t, counts, weight, moment,
    prv_all, prv_d, new_public, precond, factors,
    pub_all, pub_d, w_ref, squares, tile_squares, all_squares,
    pub_aims, prv_aims, pub_send, prv_send, pub_recv, prv_recv, pub_own, prv_own, pub_y, prv_y,
    x_recv, up_sem, down_sem, core_sem, aim_recv, aim_sent, rs_recv, rs_sent, ag_recv, ag_sent,
    tile_recv, tile_sent, all_recv, all_sent,
):
    replicas = lax.axis_size("replica")
    tiles = lax.axis_size("tile")
    r = lax.axis_index("replica")
    t = lax.axis_index("tile")
    chips = replicas // CORES
    z = r // CORES
    c = r % CORES
    cols = w_ref.shape[1]
    inner = jnp.minimum(z, chips - 1 - z)
    phases = (
        (pub_x, pub_t, pub_all, pub_d, pub_aims, pub_send, pub_recv, pub_own, pub_y),
        (prv_x, prv_t, prv_all, prv_d, prv_aims, prv_send, prv_recv, prv_own, prv_y),
    )

    pieces = pieces_of(pub_all.shape[2], prv_all.shape[2])
    last = len(pieces) - 1

    def run(f):
        return pl.ds(pieces[f][1], pieces[f][2])

    def side(f):
        return phases[pieces[f][0]]

    def to(src, dst, sent, got, replica, tile):
        return pltpu.make_async_remote_copy(
            src_ref=src, dst_ref=dst, send_sem=sent, recv_sem=got,
            device_id=(replica, tile), device_id_type=MESH,
        )

    def chip_at(i):
        k = (i + 1) // 2
        longer = jnp.where(z < chips - 1 - z, 1, -1)
        paired = jnp.where(i % 2 == 1, z + longer * k, z - longer * k)
        rest = z + longer * (i - inner)
        return jnp.where(i <= 2 * inner, paired, rest)

    def token_copy(f, q, sent, replica):
        ref = side(f)[2].at[q, :, run(f)]
        return to(ref, ref, sent, x_recv.at[f, q], replica, t)

    def aim_copy(f, d):
        other = (r + d) % replicas
        ref = phases[f][1].at[:, pl.ds(pl.multiple_of(other * cols, cols), cols)]
        return to(ref, phases[f][4].at[d - 1], aim_sent.at[f, d - 1], aim_recv.at[f, d - 1], other, t)

    def part_copy(f, q, d):
        there = (t + d) % tiles
        return to(
            side(f)[5].at[q, there, run(f)], side(f)[6].at[q, d - 1, run(f)],
            rs_sent.at[f, q, d - 1], rs_recv.at[f, q, d - 1], r, there,
        )

    def error_copy(f, q, d):
        there = (t + d) % tiles
        ref = side(f)[3].at[q, t, run(f)]
        return to(ref, ref, ag_sent.at[f, q, d - 1], ag_recv.at[f, q, d - 1], r, there)

    def error_arrival(f, q, d):
        ref = side(f)[3].at[q, (t + tiles - d) % tiles, run(f)]
        return to(ref, ref, ag_sent.at[f, q, d - 1], ag_recv.at[f, q, d - 1], r, (t + tiles - d) % tiles)

    barrier = pltpu.get_barrier_semaphore()
    for d in range(1, replicas):
        pl.semaphore_signal(barrier, inc=1, device_id=((r + d) % replicas, t), device_id_type=MESH)
    for d in range(1, tiles):
        pl.semaphore_signal(barrier, inc=1, device_id=(r, (t + d) % tiles), device_id_type=MESH)
    pub_all[r] = pub_x[...]
    examples = counts.shape[1]
    sub = prv_x.shape[1]
    seq_len = tiles * sub // examples
    for at in range(tiles):
        slot = at * sub + lax.broadcasted_iota(jnp.int32, (sub, 1), 0)
        live = jnp.zeros((sub, 1), jnp.float32)
        for e in range(examples):
            first = e * seq_len
            inside = jnp.logical_and(slot >= first, slot < first + counts[0, e])
            live = jnp.where(inside, 1.0, live)
        prv_all[r, at] = (prv_x[at].astype(jnp.float32) * live).astype(jnp.bfloat16)
    w_ref[...] = weight[...].astype(jnp.bfloat16)
    pl.semaphore_wait(barrier, replicas + tiles - 2)

    def along(f, i, chip):
        mine = chip * CORES + c

        @pl.when(jnp.logical_and(chip <= z, z < chips - 1))
        def _():
            token_copy(f, mine, up_sem.at[f, i], r + CORES).start()

        @pl.when(jnp.logical_and(chip >= z, z > 0))
        def _():
            token_copy(f, mine, down_sem.at[f, i], r - CORES).start()

    def along_done(f, i):
        chip = chip_at(i)
        mine = chip * CORES + c

        @pl.when(jnp.logical_and(chip <= z, z < chips - 1))
        def _():
            token_copy(f, mine, up_sem.at[f, i], r + CORES).wait_send()

        @pl.when(jnp.logical_and(chip >= z, z > 0))
        def _():
            token_copy(f, mine, down_sem.at[f, i], r - CORES).wait_send()

    def partial(f, q):
        _, _, x_all, _, _, send, _, own, y = side(f)
        _, first, count = pieces[f]
        stop = first + count
        tokens = dense([x_all[q, at, first:stop] for at in range(tiles)])
        out = jnp.dot(tokens, w_ref[...], preferred_element_type=jnp.float32)
        for at in range(tiles):
            part = out[at * count : (at + 1) * count]
            y[at, first:stop] = part
            send[q, at, first:stop] = part.astype(jnp.bfloat16)
        for d in range(1, tiles):
            part_copy(f, q, d).start()
        own[q, first:stop] = y[t, first:stop]

    def finish(f, q):
        _, targets, _, d_all, aims, _, recv, own, _ = side(f)
        a, first, count = pieces[f]
        stop = first + count
        gap = (r + replicas - q) % replicas

        @pl.when(gap > 0)
        def _():
            if first == 0:
                to(aims.at[gap - 1], aims.at[gap - 1], aim_sent.at[a, gap - 1], aim_recv.at[a, gap - 1], q, t).wait_recv()
            own[q, first:stop] = own[q, first:stop] - aims[gap - 1, first:stop].astype(jnp.float32)

        @pl.when(gap == 0)
        def _():
            mine = targets[first:stop, pl.ds(pl.multiple_of(r * cols, cols), cols)]
            own[q, first:stop] = own[q, first:stop] - mine.astype(jnp.float32)

        total = own[q, first:stop]
        for d in range(1, tiles):
            part_copy(f, q, d).wait_recv()
            total = total + recv[q, d - 1, first:stop].astype(jnp.float32)
        d_all[q, t, first:stop] = total.astype(jnp.bfloat16)
        for d in range(1, tiles):
            error_copy(f, q, d).start()

    def finish_chip(f, chip):
        finish(f, chip * CORES + c)
        finish(f, chip * CORES + 1 - c)

    def arrived(f, q):
        for d in range(1, tiles):
            error_arrival(f, q, d).wait_recv()

    rows = weight.shape[0]
    step = 256 if rows % 256 == 0 else rows

    def public_update():
        def waiting(q, carry):
            arrived(0, q)
            return carry

        lax.fori_loop(0, replicas, waiting, 0)
        total = replicas * tiles * pub_x.shape[1]
        errors = pub_d[...].reshape(total, cols)
        for at in range(0, rows, step):
            tokens = pub_all[:, :, :, at : at + step].reshape(total, step)
            grads = lax.dot_general(tokens, errors, contract_rows, preferred_element_type=jnp.float32)
            grads = grads * (1.0 / root)
            moved = beta_public * moment[at : at + step, :] + (1.0 - beta_public) * grads * grads
            new_public[at : at + step, :] = moved
            precond[at : at + step, :] = 1.0 / (jnp.sqrt(moved) + public_epsilon)

    def norms(chip):
        def body(which, carry):
            q = chip * CORES + (c + which) % CORES
            for f in range(1, last + 1):
                arrived(f, q)
            errors = dense([prv_d[q, at] for at in range(tiles)])
            totals = [jnp.zeros((8, cols), jnp.float32)] * examples
            for at in range(0, rows, step):
                tokens = dense([prv_all[q, own_rows, :, at : at + step] for own_rows in range(tiles)])
                for e in range(examples):
                    span = slice(e * seq_len, (e + 1) * seq_len)
                    grads = lax.dot_general(
                        tokens[span], errors[span], contract_rows, preferred_element_type=jnp.float32
                    )
                    scaled = grads * precond[at : at + step, :]
                    totals[e] = totals[e] + jnp.sum((scaled * scaled).reshape(step // 8, 8, cols), axis=0)
            for e in range(examples):
                line = jnp.sum(totals[e], axis=0, keepdims=True)
                line = sum(line[:, at : at + 128] for at in range(0, cols, 128))
                squares[pl.ds(q * examples + e, 1), :] = line
            return carry

        lax.fori_loop(0, CORES, body, 0)

    def tile_copy(d):
        return to(squares, tile_squares.at[d - 1], tile_sent.at[d - 1], tile_recv.at[d - 1], r, (t + d) % tiles)

    def all_copy(d):
        return to(
            factors, all_squares.at[d - 1], all_sent.at[d - 1], all_recv.at[d - 1], (r + d) % replicas, t
        )

    def phase(f):
        def body(i, carry):
            @pl.when(i < chips)
            def _():
                chip = chip_at(i)
                mine = chip * CORES + c
                other = chip * CORES + 1 - c

                @pl.when(i > 0)
                def _():
                    token_copy(f, mine, up_sem.at[f, i], r).wait_recv()

                if f == 0:
                    along(f, i, chip)
                else:
                    @pl.when(i > 0)
                    def _():
                        along(f, i, chip)
                token_copy(f, mine, core_sem.at[f, i], z * CORES + 1 - c).start()

                if pieces[f][1] == 0:
                    @pl.when(i == 0)
                    def _():
                        for d in range(1, replicas):
                            aim_copy(pieces[f][0], d).start()

                if f < last:
                    @pl.when(i == min(1, chips - 1))
                    def _():
                        along(f + 1, 0, z)

                partial(f, mine)
                token_copy(f, other, core_sem.at[f, i], r).wait_recv()
                partial(f, other)

            if f > 0:
                @pl.when(i == 0)
                def _():
                    finish_chip(f - 1, chip_at(chips - 1))

            @pl.when(jnp.logical_and(i > 0, i <= chips))
            def _():
                finish_chip(f, chip_at(i - 1))

            if f == 1:
                @pl.when(i == 1)
                def _():
                    public_update()

            if f == last:
                @pl.when(i > 1)
                def _():
                    norms(chip_at(i - 2))

            return carry

        lax.fori_loop(0, chips + 2 if f == last else chips, body, 0)

    for f in range(last + 1):
        phase(f)

    for d in range(1, tiles):
        tile_copy(d).start()
    for d in range(1, tiles):
        tile_copy(d).wait_recv()
    total = squares[...]
    for d in range(1, tiles):
        total = total + tile_squares[d - 1]
    factors[...] = total
    for d in range(1, replicas):
        all_copy(d).start()
    for d in range(1, replicas):
        all_copy(d).wait()
    for d in range(1, replicas):
        total = total + all_squares[d - 1]
    total = jnp.sum(total, axis=1, keepdims=True)
    factor = clip_norm / jnp.maximum(jnp.sqrt(total), clip_norm)
    factors[...] = jnp.broadcast_to(factor, factors.shape)
    for d in range(1, tiles):
        tile_copy(d).wait_send()

    def close(f):
        def body(q, carry):
            for d in range(1, tiles):
                error_copy(f, q, d).wait_send()
                part_copy(f, q, d).wait_send()
            return carry

        lax.fori_loop(0, replicas, body, 0)

        def sent(i, carry):
            along_done(f, i)
            token_copy(f, chip_at(i) * CORES + c, core_sem.at[f, i], r).wait_send()
            return carry

        lax.fori_loop(0, chips, sent, 0)
        if pieces[f][1] == 0:
            for d in range(1, replicas):
                aim_copy(pieces[f][0], d).wait_send()

    for f in range(last + 1):
        close(f)


def gathered_errors(pub_x, prv_x, pub_t, prv_t, counts, weight, moment, root, clip_norm):
    replicas = lax.axis_size("replica")
    tiles = lax.axis_size("tile")
    chips = replicas // CORES
    rows, cols = weight.shape
    half, full = jnp.bfloat16, jnp.float32
    spans = (pub_x.shape[0], prv_x.shape[0])
    subs = [span // tiles for span in spans]
    examples = counts.shape[1] * replicas
    vmem = pl.BlockSpec(memory_space=pltpu.VMEM)
    tokens = [(replicas, tiles, sub, rows) for sub in subs]
    count = len(pieces_of(*subs))
    errors = [(replicas, tiles, sub, cols) for sub in subs]
    scratch = [pltpu.VMEM(tokens[0], half), pltpu.VMEM(errors[0], half), pltpu.VMEM((rows, cols), half)]
    scratch += [pltpu.VMEM(shape + (examples, 128), full) for shape in ((), (tiles - 1,), (replicas - 1,))]
    scratch += [pltpu.VMEM((replicas - 1, sub, cols), half) for sub in subs]
    scratch += [pltpu.VMEM((replicas, tiles, sub, cols), half) for sub in subs]
    scratch += [pltpu.VMEM((replicas, tiles - 1, sub, cols), half) for sub in subs]
    scratch += [pltpu.VMEM((replicas, sub, cols), full) for sub in subs]
    scratch += [pltpu.VMEM((tiles, sub, cols), full) for sub in subs]
    sems = [(count, replicas)] + [(count, chips)] * 3 + [(2, replicas - 1)] * 2
    sems += [(count, replicas, tiles - 1)] * 4
    sems += [(tiles - 1,)] * 2 + [(replicas - 1,)] * 2
    scratch += [pltpu.SemaphoreType.DMA(shape) for shape in sems]
    flops = 4 * replicas * sum(spans) * rows * cols
    state = jax.ShapeDtypeStruct((rows, cols), full)
    return pl.pallas_call(
        functools.partial(errors_kernel, root, clip_norm),
        out_shape=[
            jax.ShapeDtypeStruct(tokens[1], half),
            jax.ShapeDtypeStruct(errors[1], half),
            state,
            state,
            jax.ShapeDtypeStruct((examples, 128), full),
        ],
        in_specs=[vmem] * 4 + [pl.BlockSpec(memory_space=pltpu.SMEM)] + [vmem] * 2,
        out_specs=[vmem] * 5,
        scratch_shapes=scratch,
        compiler_params=pltpu.CompilerParams(
            collective_id=0, has_side_effects=True, vmem_limit_bytes=58 * 1024 * 1024
        ),
        cost_estimate=pl.CostEstimate(flops=flops, bytes_accessed=2 * replicas * sum(spans) * rows, transcendentals=0),
        name="gathered_errors",
    )(
        pub_x.reshape(tiles, subs[0], rows), prv_x.reshape(tiles, subs[1], rows),
        pub_t, prv_t, counts, weight, moment,
    )


def update_kernel(
    total_examples, noise_scale, f_ref, x_ref, d_ref, p_ref, n_ref, m_ref, v_ref, w_ref,
    new_w, new_m, new_v, weighted,
):
    examples = f_ref.shape[0]
    seq_len = d_ref.shape[0] // examples

    @pl.when(pl.program_id(0) == 0)
    def _():
        for j in range(examples):
            at = slice(j * seq_len, (j + 1) * seq_len)
            weighted[at, :] = (f_ref[j : j + 1, :1] * d_ref[at, :].astype(jnp.float32)).astype(jnp.bfloat16)

    summed = p_ref[...] * lax.dot_general(
        x_ref[...], weighted[...], contract_rows, preferred_element_type=jnp.float32
    )
    gradient = (summed + noise_scale * n_ref[...]) * (1.0 / total_examples)
    first = beta_first * m_ref[...] + (1.0 - beta_first) * gradient
    second = beta_second * v_ref[...] + (1.0 - beta_second) * gradient * gradient
    new_m[...] = first
    new_v[...] = second
    first_hat = first * (1.0 / (1.0 - beta_first**2))
    second_hat = second * (1.0 / (1.0 - beta_second**2))
    new_w[...] = w_ref[...] - learn_rate * first_hat / (jnp.sqrt(second_hat) + adam_epsilon)


def update(factors, tokens, delta, precond, noise, first, second, weight, noise_scale):
    slots, rows = tokens.shape
    cols = delta.shape[1]
    examples = factors.shape[0]
    step = 256 if rows % 256 == 0 else rows
    state = pl.BlockSpec((step, cols), lambda i: (i, 0))
    return pl.pallas_call(
        functools.partial(update_kernel, examples, noise_scale),
        grid=(rows // step,),
        in_specs=[
            pl.BlockSpec((examples, 128), lambda i: (0, 0)),
            pl.BlockSpec((slots, step), lambda i: (0, i)),
            pl.BlockSpec((slots, cols), lambda i: (0, 0)),
        ]
        + [state] * 5,
        out_specs=[state] * 3,
        out_shape=[jax.ShapeDtypeStruct((rows, cols), jnp.float32)] * 3,
        scratch_shapes=[pltpu.VMEM((slots, cols), jnp.bfloat16)],
        compiler_params=pltpu.CompilerParams(vmem_limit_bytes=48 * 1024 * 1024),
        cost_estimate=pl.CostEstimate(
            flops=2 * slots * rows * cols,
            bytes_accessed=2 * slots * (rows + cols) + 32 * rows * cols,
            transcendentals=rows * cols,
        ),
        name="update",
    )(factors, tokens, delta, precond, noise, first, second, weight)


def on_device(
    public_tokens,
    public_targets,
    private_tokens,
    private_targets,
    token_counts,
    weight,
    public_moment,
    adam_first,
    adam_second,
    noise_draw,
):
    replicas = lax.axis_size("replica")
    tiles = lax.axis_size("tile")
    examples_here = token_counts.shape[1]
    slots_here = private_tokens.shape[0]
    seq_len = slots_here // examples_here
    width = weight.shape[0] * tiles
    columns = weight.shape[1] * replicas
    cols = weight.shape[1]
    public_total = public_tokens.shape[0] * replicas

    clip_norm = clip_factor * math.sqrt(seq_len * width * columns)
    private_all, private_delta, new_public, precond, factors = gathered_errors(
        public_tokens, private_tokens, public_targets, private_targets, token_counts, weight, public_moment,
        math.sqrt(public_total), clip_norm,
    )
    private_all = private_all.reshape(slots_here * replicas, -1)
    private_delta = private_delta.reshape(slots_here * replicas, cols)
    noise_scale = noise_level * clip_factor * math.sqrt(seq_len)
    new_weight, new_first, new_second = update(
        factors, private_all, private_delta, precond, noise_draw, adam_first, adam_second, weight, noise_scale
    )
    return (new_weight, new_first, new_second, new_public)


def solution(mesh):
    placed = (
        P("replica", "tile"),
        P(("replica", "tile"), None),
        P("replica", "tile"),
        P(("replica", "tile"), None),
        P("replica", None),
        P("tile", "replica"),
        P("tile", "replica"),
        P("tile", "replica"),
        P("tile", "replica"),
        P("tile", "replica"),
    )
    return jax.shard_map(
        on_device,
        mesh=mesh,
        in_specs=placed,
        out_specs=(
            P("tile", "replica"),
            P("tile", "replica"),
            P("tile", "replica"),
            P("tile", "replica"),
        ),
        check_vma=False,
    )
```

```python
import functools
import math

import jax
import jax.numpy as jnp
from jax import lax
from jax.experimental import pallas as pl
from jax.experimental.pallas import tpu as pltpu
from jax.sharding import PartitionSpec as P

beta_first = 0.9
beta_second = 0.99
beta_public = 0.9
public_epsilon = 0.001
adam_epsilon = 1e-08
clip_factor = 0.6
noise_level = 4.0
learn_rate = 0.01
contract_rows = (((0,), (0,)), ((), ()))


MESH = pl.DeviceIdType.MESH
CORES = 2


def pieces_of(public_rows, private_rows):
    cut = 3 if private_rows % 48 == 0 else 1
    private = private_rows // cut
    return [(0, 0, public_rows)] + [(1, at * private, private) for at in range(cut)]


def dense(parts):
    if parts[0].shape[0] % 16 == 0:
        return jnp.concatenate(parts, axis=0)
    return jnp.concatenate([part.astype(jnp.float32) for part in parts], axis=0).astype(parts[0].dtype)


def errors_kernel(
    root, clip_norm,
    pub_x, prv_x, pub_t, prv_t, counts, weight, moment,
    prv_all, prv_d, new_public, factors,
    pub_all, pub_d, w_ref, precond, squares, tile_squares, all_squares,
    pub_aims, prv_aims, pub_send, prv_send, pub_recv, prv_recv, pub_own, prv_own, pub_y, prv_y,
    x_recv, up_sem, down_sem, core_sem, aim_recv, aim_sent, rs_recv, rs_sent, ag_recv, ag_sent,
    tile_recv, tile_sent, all_recv, all_sent,
):
    replicas = lax.axis_size("replica")
    tiles = lax.axis_size("tile")
    r = lax.axis_index("replica")
    t = lax.axis_index("tile")
    chips = replicas // CORES
    z = r // CORES
    c = r % CORES
    cols = w_ref.shape[1]
    inner = jnp.minimum(z, chips - 1 - z)
    phases = (
        (pub_x, pub_t, pub_all, pub_d, pub_aims, pub_send, pub_recv, pub_own, pub_y),
        (prv_x, prv_t, prv_all, prv_d, prv_aims, prv_send, prv_recv, prv_own, prv_y),
    )

    pieces = pieces_of(pub_all.shape[2], prv_all.shape[2])
    last = len(pieces) - 1

    def run(f):
        return pl.ds(pieces[f][1], pieces[f][2])

    def side(f):
        return phases[pieces[f][0]]

    def to(src, dst, sent, got, replica, tile):
        return pltpu.make_async_remote_copy(
            src_ref=src, dst_ref=dst, send_sem=sent, recv_sem=got,
            device_id=(replica, tile), device_id_type=MESH,
        )

    def chip_at(i):
        k = (i + 1) // 2
        longer = jnp.where(z < chips - 1 - z, 1, -1)
        paired = jnp.where(i % 2 == 1, z + longer * k, z - longer * k)
        rest = z + longer * (i - inner)
        return jnp.where(i <= 2 * inner, paired, rest)

    def token_copy(f, q, sent, replica):
        ref = side(f)[2].at[q, :, run(f)]
        return to(ref, ref, sent, x_recv.at[f, q], replica, t)

    def aim_copy(f, d):
        other = (r + d) % replicas
        ref = phases[f][1].at[:, pl.ds(pl.multiple_of(other * cols, cols), cols)]
        return to(ref, phases[f][4].at[d - 1], aim_sent.at[f, d - 1], aim_recv.at[f, d - 1], other, t)

    def part_copy(f, q, d):
        there = (t + d) % tiles
        return to(
            side(f)[5].at[q, there, run(f)], side(f)[6].at[q, d - 1, run(f)],
            rs_sent.at[f, q, d - 1], rs_recv.at[f, q, d - 1], r, there,
        )

    def error_copy(f, q, d):
        there = (t + d) % tiles
        ref = side(f)[3].at[q, t, run(f)]
        return to(ref, ref, ag_sent.at[f, q, d - 1], ag_recv.at[f, q, d - 1], r, there)

    def error_arrival(f, q, d):
        ref = side(f)[3].at[q, (t + tiles - d) % tiles, run(f)]
        return to(ref, ref, ag_sent.at[f, q, d - 1], ag_recv.at[f, q, d - 1], r, (t + tiles - d) % tiles)

    barrier = pltpu.get_barrier_semaphore()
    for d in range(1, replicas):
        pl.semaphore_signal(barrier, inc=1, device_id=((r + d) % replicas, t), device_id_type=MESH)
    for d in range(1, tiles):
        pl.semaphore_signal(barrier, inc=1, device_id=(r, (t + d) % tiles), device_id_type=MESH)
    pub_all[r] = pub_x[...]
    examples = counts.shape[1]
    sub = prv_x.shape[1]
    seq_len = tiles * sub // examples
    for at in range(tiles):
        slot = at * sub + lax.broadcasted_iota(jnp.int32, (sub, 1), 0)
        live = jnp.zeros((sub, 1), jnp.float32)
        for e in range(examples):
            first = e * seq_len
            inside = jnp.logical_and(slot >= first, slot < first + counts[0, e])
            live = jnp.where(inside, 1.0, live)
        prv_all[r, at] = (prv_x[at].astype(jnp.float32) * live).astype(jnp.bfloat16)
    w_ref[...] = weight[...].astype(jnp.bfloat16)
    pl.semaphore_wait(barrier, replicas + tiles - 2)

    def along(f, i, chip):
        mine = chip * CORES + c

        @pl.when(jnp.logical_and(chip <= z, z < chips - 1))
        def _():
            token_copy(f, mine, up_sem.at[f, i], r + CORES).start()

        @pl.when(jnp.logical_and(chip >= z, z > 0))
        def _():
            token_copy(f, mine, down_sem.at[f, i], r - CORES).start()

    def along_done(f, i):
        chip = chip_at(i)
        mine = chip * CORES + c

        @pl.when(jnp.logical_and(chip <= z, z < chips - 1))
        def _():
            token_copy(f, mine, up_sem.at[f, i], r + CORES).wait_send()

        @pl.when(jnp.logical_and(chip >= z, z > 0))
        def _():
            token_copy(f, mine, down_sem.at[f, i], r - CORES).wait_send()

    def partial(f, q):
        _, _, x_all, _, _, send, _, own, y = side(f)
        _, first, count = pieces[f]
        stop = first + count
        tokens = dense([x_all[q, at, first:stop] for at in range(tiles)])
        out = jnp.dot(tokens, w_ref[...], preferred_element_type=jnp.float32)
        for at in range(tiles):
            part = out[at * count : (at + 1) * count]
            y[at, first:stop] = part
            send[q, at, first:stop] = part.astype(jnp.bfloat16)
        for d in range(1, tiles):
            part_copy(f, q, d).start()
        own[q, first:stop] = y[t, first:stop]

    def finish(f, q):
        _, targets, _, d_all, aims, _, recv, own, _ = side(f)
        a, first, count = pieces[f]
        stop = first + count
        gap = (r + replicas - q) % replicas

        @pl.when(gap > 0)
        def _():
            if first == 0:
                to(aims.at[gap - 1], aims.at[gap - 1], aim_sent.at[a, gap - 1], aim_recv.at[a, gap - 1], q, t).wait_recv()
            own[q, first:stop] = own[q, first:stop] - aims[gap - 1, first:stop].astype(jnp.float32)

        @pl.when(gap == 0)
        def _():
            mine = targets[first:stop, pl.ds(pl.multiple_of(r * cols, cols), cols)]
            own[q, first:stop] = own[q, first:stop] - mine.astype(jnp.float32)

        total = own[q, first:stop]
        for d in range(1, tiles):
            part_copy(f, q, d).wait_recv()
            total = total + recv[q, d - 1, first:stop].astype(jnp.float32)
        d_all[q, t, first:stop] = total.astype(jnp.bfloat16)
        for d in range(1, tiles):
            error_copy(f, q, d).start()

    def finish_chip(f, chip):
        finish(f, chip * CORES + c)
        finish(f, chip * CORES + 1 - c)

    def arrived(f, q):
        for d in range(1, tiles):
            error_arrival(f, q, d).wait_recv()

    rows = weight.shape[0]
    step = 256 if rows % 256 == 0 else rows

    def public_update():
        def waiting(q, carry):
            arrived(0, q)
            return carry

        lax.fori_loop(0, replicas, waiting, 0)
        total = replicas * tiles * pub_x.shape[1]
        errors = pub_d[...].reshape(total, cols)
        for at in range(0, rows, step):
            tokens = pub_all[:, :, :, at : at + step].reshape(total, step)
            grads = lax.dot_general(tokens, errors, contract_rows, preferred_element_type=jnp.float32)
            grads = grads * (1.0 / root)
            moved = beta_public * moment[at : at + step, :] + (1.0 - beta_public) * grads * grads
            new_public[at : at + step, :] = moved
            precond[at : at + step, :] = 1.0 / (jnp.sqrt(moved) + public_epsilon)

    def norms(chip):
        def body(which, carry):
            q = chip * CORES + (c + which) % CORES
            for f in range(1, last + 1):
                arrived(f, q)
            errors = dense([prv_d[q, at] for at in range(tiles)])
            totals = [jnp.zeros((8, cols), jnp.float32)] * examples
            for at in range(0, rows, step):
                tokens = dense([prv_all[q, own_rows, :, at : at + step] for own_rows in range(tiles)])
                for e in range(examples):
                    span = slice(e * seq_len, (e + 1) * seq_len)
                    grads = lax.dot_general(
                        tokens[span], errors[span], contract_rows, preferred_element_type=jnp.float32
                    )
                    scaled = grads * precond[at : at + step, :]
                    totals[e] = totals[e] + jnp.sum((scaled * scaled).reshape(step // 8, 8, cols), axis=0)
            for e in range(examples):
                line = jnp.sum(totals[e], axis=0, keepdims=True)
                line = sum(line[:, at : at + 128] for at in range(0, cols, 128))
                squares[pl.ds(q * examples + e, 1), :] = line
            return carry

        lax.fori_loop(0, CORES, body, 0)

    def tile_copy(d):
        return to(squares, tile_squares.at[d - 1], tile_sent.at[d - 1], tile_recv.at[d - 1], r, (t + d) % tiles)

    def all_copy(d):
        return to(
            factors, all_squares.at[d - 1], all_sent.at[d - 1], all_recv.at[d - 1], (r + d) % replicas, t
        )

    def phase(f):
        def body(i, carry):
            @pl.when(i < chips)
            def _():
                chip = chip_at(i)
                mine = chip * CORES + c
                other = chip * CORES + 1 - c

                @pl.when(i > 0)
                def _():
                    token_copy(f, mine, up_sem.at[f, i], r).wait_recv()

                if f == 0:
                    along(f, i, chip)
                else:
                    @pl.when(i > 0)
                    def _():
                        along(f, i, chip)
                token_copy(f, mine, core_sem.at[f, i], z * CORES + 1 - c).start()

                if pieces[f][1] == 0:
                    @pl.when(i == 0)
                    def _():
                        for d in range(1, replicas):
                            aim_copy(pieces[f][0], d).start()

                ahead = [g for g in ((1, 2) if f == 0 else (f + 2,)) if g <= last]
                if ahead:
                    @pl.when(i == min(1, chips - 1))
                    def _():
                        for g in ahead:
                            along(g, 0, z)

                partial(f, mine)
                token_copy(f, other, core_sem.at[f, i], r).wait_recv()
                partial(f, other)

            if f > 0:
                @pl.when(i == 0)
                def _():
                    finish_chip(f - 1, chip_at(chips - 1))

            @pl.when(jnp.logical_and(i > 0, i <= chips))
            def _():
                finish_chip(f, chip_at(i - 1))

            if f == 1:
                @pl.when(i == 1)
                def _():
                    public_update()

            if f == last:
                @pl.when(i > 1)
                def _():
                    norms(chip_at(i - 2))

            return carry

        lax.fori_loop(0, chips + 2 if f == last else chips, body, 0)

    for f in range(last + 1):
        phase(f)

    for d in range(1, tiles):
        tile_copy(d).start()
    for d in range(1, tiles):
        tile_copy(d).wait_recv()
    total = squares[...]
    for d in range(1, tiles):
        total = total + tile_squares[d - 1]
    factors[...] = total
    for d in range(1, replicas):
        all_copy(d).start()
    for d in range(1, replicas):
        all_copy(d).wait()
    for d in range(1, replicas):
        total = total + all_squares[d - 1]
    total = jnp.sum(total, axis=1, keepdims=True)
    factor = clip_norm / jnp.maximum(jnp.sqrt(total), clip_norm)
    factors[...] = jnp.broadcast_to(factor, factors.shape)
    for d in range(1, tiles):
        tile_copy(d).wait_send()

    def close(f):
        def body(q, carry):
            for d in range(1, tiles):
                error_copy(f, q, d).wait_send()
                part_copy(f, q, d).wait_send()
            return carry

        lax.fori_loop(0, replicas, body, 0)

        def sent(i, carry):
            along_done(f, i)
            token_copy(f, chip_at(i) * CORES + c, core_sem.at[f, i], r).wait_send()
            return carry

        lax.fori_loop(0, chips, sent, 0)
        if pieces[f][1] == 0:
            for d in range(1, replicas):
                aim_copy(pieces[f][0], d).wait_send()

    for f in range(last + 1):
        close(f)


def gathered_errors(pub_x, prv_x, pub_t, prv_t, counts, weight, moment, root, clip_norm):
    replicas = lax.axis_size("replica")
    tiles = lax.axis_size("tile")
    chips = replicas // CORES
    rows, cols = weight.shape
    half, full = jnp.bfloat16, jnp.float32
    spans = (pub_x.shape[0], prv_x.shape[0])
    subs = [span // tiles for span in spans]
    examples = counts.shape[1] * replicas
    vmem = pl.BlockSpec(memory_space=pltpu.VMEM)
    tokens = [(replicas, tiles, sub, rows) for sub in subs]
    count = len(pieces_of(*subs))
    errors = [(replicas, tiles, sub, cols) for sub in subs]
    scratch = [pltpu.VMEM(tokens[0], half), pltpu.VMEM(errors[0], half), pltpu.VMEM((rows, cols), half)]
    scratch += [pltpu.VMEM((rows, cols), full)]
    scratch += [pltpu.VMEM(shape + (examples, 128), full) for shape in ((), (tiles - 1,), (replicas - 1,))]
    scratch += [pltpu.VMEM((replicas - 1, sub, cols), half) for sub in subs]
    scratch += [pltpu.VMEM((replicas, tiles, sub, cols), half) for sub in subs]
    scratch += [pltpu.VMEM((replicas, tiles - 1, sub, cols), half) for sub in subs]
    scratch += [pltpu.VMEM((replicas, sub, cols), full) for sub in subs]
    scratch += [pltpu.VMEM((tiles, sub, cols), full) for sub in subs]
    sems = [(count, replicas)] + [(count, chips)] * 3 + [(2, replicas - 1)] * 2
    sems += [(count, replicas, tiles - 1)] * 4
    sems += [(tiles - 1,)] * 2 + [(replicas - 1,)] * 2
    scratch += [pltpu.SemaphoreType.DMA(shape) for shape in sems]
    flops = 4 * replicas * sum(spans) * rows * cols
    state = jax.ShapeDtypeStruct((rows, cols), full)
    return pl.pallas_call(
        functools.partial(errors_kernel, root, clip_norm),
        out_shape=[
            jax.ShapeDtypeStruct(tokens[1], half),
            jax.ShapeDtypeStruct(errors[1], half),
            state,
            jax.ShapeDtypeStruct((examples, 128), full),
        ],
        in_specs=[vmem] * 4 + [pl.BlockSpec(memory_space=pltpu.SMEM)] + [vmem] * 2,
        out_specs=[vmem] * 4,
        scratch_shapes=scratch,
        compiler_params=pltpu.CompilerParams(
            collective_id=0, has_side_effects=True, vmem_limit_bytes=58 * 1024 * 1024
        ),
        cost_estimate=pl.CostEstimate(flops=flops, bytes_accessed=2 * replicas * sum(spans) * rows, transcendentals=0),
        name="gathered_errors",
    )(
        pub_x.reshape(tiles, subs[0], rows), prv_x.reshape(tiles, subs[1], rows),
        pub_t, prv_t, counts, weight, moment,
    )


def update_kernel(
    total_examples, noise_scale, f_ref, x_ref, d_ref, p_ref, n_ref, m_ref, v_ref, w_ref,
    new_w, new_m, new_v, new_p, weighted,
):
    examples = f_ref.shape[0]
    seq_len = d_ref.shape[0] // examples

    @pl.when(pl.program_id(0) == 0)
    def _():
        for j in range(examples):
            at = slice(j * seq_len, (j + 1) * seq_len)
            weighted[at, :] = (f_ref[j : j + 1, :1] * d_ref[at, :].astype(jnp.float32)).astype(jnp.bfloat16)

    new_p[...] = p_ref[...]
    precond = 1.0 / (jnp.sqrt(p_ref[...]) + public_epsilon)
    summed = precond * lax.dot_general(
        x_ref[...], weighted[...], contract_rows, preferred_element_type=jnp.float32
    )
    gradient = (summed + noise_scale * n_ref[...]) * (1.0 / total_examples)
    first = beta_first * m_ref[...] + (1.0 - beta_first) * gradient
    second = beta_second * v_ref[...] + (1.0 - beta_second) * gradient * gradient
    new_m[...] = first
    new_v[...] = second
    first_hat = first * (1.0 / (1.0 - beta_first**2))
    second_hat = second * (1.0 / (1.0 - beta_second**2))
    new_w[...] = w_ref[...] - learn_rate * first_hat / (jnp.sqrt(second_hat) + adam_epsilon)


def update(factors, tokens, delta, public, noise, first, second, weight, noise_scale):
    slots, rows = tokens.shape
    cols = delta.shape[1]
    examples = factors.shape[0]
    step = 256 if rows % 256 == 0 else rows
    state = pl.BlockSpec((step, cols), lambda i: (i, 0))
    return pl.pallas_call(
        functools.partial(update_kernel, examples, noise_scale),
        grid=(rows // step,),
        in_specs=[
            pl.BlockSpec((examples, 128), lambda i: (0, 0)),
            pl.BlockSpec((slots, step), lambda i: (0, i)),
            pl.BlockSpec((slots, cols), lambda i: (0, 0)),
        ]
        + [state] * 5,
        out_specs=[state] * 4,
        out_shape=[jax.ShapeDtypeStruct((rows, cols), jnp.float32)] * 4,
        scratch_shapes=[pltpu.VMEM((slots, cols), jnp.bfloat16)],
        compiler_params=pltpu.CompilerParams(vmem_limit_bytes=48 * 1024 * 1024),
        cost_estimate=pl.CostEstimate(
            flops=2 * slots * rows * cols,
            bytes_accessed=2 * slots * (rows + cols) + 32 * rows * cols,
            transcendentals=rows * cols,
        ),
        name="update",
    )(factors, tokens, delta, public, noise, first, second, weight)


def on_device(
    public_tokens,
    public_targets,
    private_tokens,
    private_targets,
    token_counts,
    weight,
    public_moment,
    adam_first,
    adam_second,
    noise_draw,
):
    replicas = lax.axis_size("replica")
    tiles = lax.axis_size("tile")
    examples_here = token_counts.shape[1]
    slots_here = private_tokens.shape[0]
    seq_len = slots_here // examples_here
    width = weight.shape[0] * tiles
    columns = weight.shape[1] * replicas
    cols = weight.shape[1]
    public_total = public_tokens.shape[0] * replicas

    clip_norm = clip_factor * math.sqrt(seq_len * width * columns)
    private_all, private_delta, new_public, factors = gathered_errors(
        public_tokens, private_tokens, public_targets, private_targets, token_counts, weight, public_moment,
        math.sqrt(public_total), clip_norm,
    )
    private_all = private_all.reshape(slots_here * replicas, -1)
    private_delta = private_delta.reshape(slots_here * replicas, cols)
    noise_scale = noise_level * clip_factor * math.sqrt(seq_len)
    new_weight, new_first, new_second, new_public = update(
        factors, private_all, private_delta, new_public, noise_draw, adam_first, adam_second, weight, noise_scale
    )
    return (new_weight, new_first, new_second, new_public)


def solution(mesh):
    placed = (
        P("replica", "tile"),
        P(("replica", "tile"), None),
        P("replica", "tile"),
        P(("replica", "tile"), None),
        P("replica", None),
        P("tile", "replica"),
        P("tile", "replica"),
        P("tile", "replica"),
        P("tile", "replica"),
        P("tile", "replica"),
    )
    return jax.shard_map(
        on_device,
        mesh=mesh,
        in_specs=placed,
        out_specs=(
            P("tile", "replica"),
            P("tile", "replica"),
            P("tile", "replica"),
            P("tile", "replica"),
        ),
        check_vma=False,
    )
```
